32 devices in a mesh: seq: 4 (over y, x), exp: 8 (over z, core).
Axes of the slice: x: 2, y: 2, z: 4, core: 2. Of those that a mesh axis runs over, the one named last changes fastest.
Arguments:
- tokens: bfloat16 [2048, 2560], P('exp'), may hold values from -6 to 6
- norm_gain: float32 [2560], replicated, may hold values from 0.1 to 1.9
- routes: int32 [2048, 6], P('exp'), may hold values from 0 to 15, all different within a row; in each aligned block of 256 rows (0 to 255, 256 to 511, ...) at most 97 rows name the same one
- route_weights: bfloat16 [2048, 6], P('exp'), may hold values from 0.049804688 to 0.3984375
- w_gate: bfloat16 [16, 2560, 1536], P('exp', None, 'seq'), may hold values from -0.125 to 0.125
- w_up: bfloat16 [16, 2560, 1536], P('exp', None, 'seq'), may hold values from -0.125 to 0.125
- w_down: bfloat16 [16, 1536, 2560], P('exp', 'seq'), may hold values from -0.15625 to 0.15625
- kv_prefill: bfloat16 [4, 256, 32, 1024], P(None, ('seq', 'exp')), may hold values from -6 to 6
- block_map: int32 [256], P(('seq', 'exp')), may hold values from 0 to 255, as said below
- block_empty: int32 [256], P(('seq', 'exp')), may hold values 0 or 1
Outputs:
- moe_out: bfloat16 [2048, 2560], P('exp', 'seq')
- kv_decode: bfloat16 [4, 256, 32, 1024], P(None, ('seq', 'exp'))
The draws below stay inside these ranges and needn't reach their ends.
Inputs may be any that keep to these rules, and one draw needn't show every extreme that they name: `routes`: in each aligned block of 256 rows no expert is named by more than 97 rows, a bound that some block reaches. block_map is a permutation of the 256 blocks; a block keeps its index of exp, and each device sends exactly 2 blocks to each device of its seq group, itself included.
All inputs are finite; a program needn't handle non-finite values. No bound on the sum of `block_empty` on one device may be relied on, other than what follows from the above.
Results may differ from the reference program's by a relative error of at most 0.013.
Values may be sent and summed in bfloat16 or wider, within the bound.
A program may use at most 128 MiB of HBM per device.

```python
import math
import jax
import jax.numpy as jnp
import numpy as np
from jax import lax

D = 2560
FF = 1536
TOPK = 6
TOK_DEV = 256
LAYERS_KV = 4
BLK_TOK = 32
BLK_DEV = 8
EXPERTS = 16
CAP = 97
TOKENS = 2048
KVW = 1024
NBLK = 256
N_SEQ = 4
N_EXP = 8


def draw_block_map(key, part):
    device_count = N_SEQ * N_EXP
    first_key, second_key = jax.random.split(jax.random.fold_in(key, 17))
    source_order = jax.vmap(lambda k: jax.random.permutation(k, BLK_DEV))(jax.random.split(first_key, device_count)).astype(jnp.int32)
    target_order = jax.vmap(lambda k: jax.random.permutation(k, BLK_DEV))(jax.random.split(second_key, device_count)).astype(jnp.int32)
    device = jnp.arange(device_count, dtype=jnp.int32)[:, None]
    ordinal = jnp.arange(BLK_DEV, dtype=jnp.int32)[None, :]
    seq_index = device // N_EXP
    exp_index = device % N_EXP
    target_seq = (seq_index + ordinal) % N_SEQ
    target_device = target_seq * N_EXP + exp_index
    target_slot = target_order[target_device, jnp.broadcast_to(ordinal, target_device.shape)]
    target = target_device * BLK_DEV + target_slot
    source = device * BLK_DEV + source_order
    result = jnp.zeros((device_count * BLK_DEV,), jnp.int32)
    return result.at[source.reshape(-1)].set(target.reshape(-1))


def touch_ends(entries, key, low, high):
    longest = entries.shape.index(max(entries.shape))
    spots = []
    for shift in (0, 1):
        where = [jax.random.randint(jax.random.fold_in(key, axis), (), 0, length) for axis, length in enumerate(entries.shape)]
        where[longest] = (where[longest] + shift) % entries.shape[longest]
        spots.append(tuple(where))
    return entries.at[spots[0]].set(low).at[spots[1]].set(high)


def level_of(rng, dims, cuts, low, high):
    def one(axis_at, parts):
        draws = jax.random.uniform(jax.random.fold_in(jax.random.fold_in(rng, 6), axis_at), (parts,), jnp.float32, low / len(cuts), high / len(cuts))
        return jnp.repeat(jnp.exp(draws), dims[axis_at] // parts).reshape((-1,) + (1,) * (len(dims) - axis_at - 1))

    gain = one(*cuts[0])
    for cut in cuts[1:]:
        gain = gain * one(*cut)
    return gain


def deal_out(stream_key, own, number, rows, amount, top, reach, skew):
    order = jax.random.permutation(stream_key, amount)
    heavy_load, common = portions_of(amount, rows * top, reach, skew, True), portions_of(amount, rows * top, reach, skew, False)
    places = jnp.arange(amount)

    def named(lengths, turn):
        used = int((lengths > 0).sum())
        fixed = max(1, used // 4)
        shifted = fixed + (places - fixed + turn * (used - fixed)) % max(1, amount - fixed)
        return jnp.zeros((amount,), jnp.int32).at[order[jnp.where(places < fixed, places, shifted)]].set(jnp.asarray(lengths, jnp.int32))

    lengths = jnp.where(number % 4 == 0, named(heavy_load, number // 4), named(common, number - number // 4 - 1))
    mixed = jax.random.permutation(jax.random.fold_in(own, 3), amount)
    source_of, sink = mixed[0:amount // 2 * 2:2], mixed[1:amount // 2 * 2:2]
    slack = jnp.minimum(lengths[source_of] - 1, reach - lengths[sink]) // 2
    slack = jnp.where((source_of == order[0]) | (sink == order[0]) | (lengths[sink] == 0), 0, jnp.maximum(slack, 0))
    shifted = jax.random.randint(jax.random.fold_in(own, 4), (amount // 2,), 0, 1 << 20) % (slack + 1)
    lengths = lengths.at[source_of].add(-shifted).at[sink].add(shifted)
    members = jnp.searchsorted(jnp.cumsum(lengths), jnp.arange(rows * top), side="right").astype(jnp.int32)
    table = members.reshape(top, rows).T
    table = table[jax.random.permutation(jax.random.fold_in(own, 1), rows)]
    turn = jax.random.randint(jax.random.fold_in(own, 2), (rows, 1), 0, top)
    return jnp.take_along_axis(table, (jnp.arange(top)[None, :] + turn) % top, axis=1)


def portions_of(count, total, limit, lean, full):
    weights = [(1 << 20) // math.isqrt(rank ** lean) + 1 for rank in range(1, count + 1)]
    largest = limit if full else min(limit, max(-(-total // count), total * weights[0] // sum(weights)))
    least = 1 if total - largest >= count - 1 else 0
    holding, spare = [largest] + [least] * (count - 1), total - largest - least * (count - 1)
    while spare > 0:
        movable = [i for i in range(1, count) if holding[i] < largest] or [i for i in range(1, count) if holding[i] < limit]
        mass, remaining = sum([weights[i] for i in movable]), spare
        for i in movable:
            addition = min(limit - holding[i], max(1, remaining * weights[i] // mass), spare)
            holding[i] = holding[i] + addition
            spare = spare - addition
    return np.array(holding)


def centred(stream_key, shape, width, limit, cuts=(), kind=jnp.bfloat16):
    gain = level_of(stream_key, shape, cuts, -0.22, 0.18) if cuts else 1.0
    values = jax.random.normal(stream_key, shape, jnp.float32) * width * gain
    return jnp.minimum(jnp.maximum(values, -limit), limit).astype(kind)


def setup_inputs(seed: int = 0) -> dict:
    arg_keys = jax.random.split(jax.random.key(seed), 11)
    tokens = centred(arg_keys[0], (TOKENS, D), 1.0, 6.0, ((0, 8),))
    norm_gain = jnp.clip(1.0 + 0.18 * jax.random.normal(arg_keys[1], (D,), jnp.float32), 0.1, 1.9)
    routes_keys = jax.random.split(jax.random.fold_in(arg_keys[2], 1), TOKENS // TOK_DEV)
    routes_turns = jax.random.permutation(jax.random.fold_in(arg_keys[2], 3), TOKENS // TOK_DEV)
    routes = jax.vmap(lambda own, number: deal_out(jax.random.fold_in(arg_keys[2], 2), own, number, TOK_DEV, EXPERTS, TOPK, CAP, 2))(routes_keys, routes_turns).reshape((TOKENS, TOPK))
    route_weights = jnp.clip(0.049804688 + 0.3486328 * jax.random.uniform(arg_keys[3], (TOKENS, TOPK), jnp.float32) ** level_of(arg_keys[3], (TOKENS, TOPK), ((0, 8),), -0.2, 0.2), 0.049804688, 0.3984375).astype(jnp.bfloat16)
    w_gate = centred(arg_keys[4], (EXPERTS, D, FF), D ** -0.5, 0.125, ((0, 8), (2, 4)))
    w_up = centred(arg_keys[5], (EXPERTS, D, FF), D ** -0.5, 0.125, ((0, 8), (2, 4)))
    w_down = centred(arg_keys[6], (EXPERTS, FF, D), FF ** -0.5, 0.15625, ((0, 8), (1, 4)))
    kv_prefill = centred(arg_keys[7], (LAYERS_KV, NBLK, BLK_TOK, KVW), 1.0, 6.0, ((1, 32),))
    block_map = draw_block_map(jax.random.fold_in(arg_keys[10], 71), 0)
    block_empty = touch_ends((jax.random.randint(arg_keys[9], (NBLK,), 0, 4) < 1).astype(jnp.int32), jax.random.fold_in(arg_keys[9], 1), 0, 1)
    return {"tokens": tokens, "norm_gain": norm_gain, "routes": routes, "route_weights": route_weights, "w_gate": w_gate, "w_up": w_up, "w_down": w_down, "kv_prefill": kv_prefill, "block_map": block_map, "block_empty": block_empty}


def reference(tokens, norm_gain, routes, route_weights, w_gate, w_up, w_down, kv_prefill, block_map, block_empty):
    values = tokens.astype(jnp.float32)
    scale = lax.rsqrt(lax.optimization_barrier(jnp.mean(values * values, axis=-1, keepdims=True)) + 1e-06)
    normed = (values * scale * norm_gain).astype(jnp.bfloat16)
    assigned = TOKENS * TOPK
    most_rows = CAP * N_EXP
    slice_width = FF // N_SEQ
    flat_routes = routes.reshape(-1)
    weight_table = jnp.concatenate([route_weights.reshape(-1).astype(jnp.float32), jnp.zeros((1,), jnp.float32)])
    padded = jnp.concatenate([normed, jnp.zeros((1, D), jnp.bfloat16)], axis=0)

    def one_expert(totals, expert):
        index = jnp.nonzero(flat_routes == expert, size=most_rows, fill_value=assigned)[0].astype(jnp.int32)
        token_index = index // TOPK
        rows = padded[token_index]
        gate = jnp.dot(rows, w_gate[expert], preferred_element_type=jnp.float32)
        upward = jnp.dot(rows, w_up[expert], preferred_element_type=jnp.float32)
        hidden = (jax.nn.silu(gate) * upward).astype(jnp.bfloat16)
        pieces = jnp.einsum('rsf,sfd->rsd', hidden.reshape(most_rows, N_SEQ, slice_width).astype(jnp.float32), w_down[expert].reshape(N_SEQ, slice_width, D).astype(jnp.float32), precision=lax.Precision.HIGHEST)
        rounded = lax.optimization_barrier(pieces.astype(jnp.bfloat16))
        expert_out = lax.optimization_barrier(jnp.sum(rounded.astype(jnp.float32), axis=1))
        weight = weight_table[index]
        totals = totals.at[token_index].add(expert_out * weight[:, None])
        return (totals, None)
    start = jnp.zeros((TOKENS + 1, D), jnp.float32)
    totals, unused = lax.scan(one_expert, start, jnp.arange(EXPERTS, dtype=jnp.int32))
    moe_out = totals[:TOKENS].astype(jnp.bfloat16)
    keep = (1 - block_empty).astype(kv_prefill.dtype)
    kept = kv_prefill * keep[None, :, None, None]
    kv_decode = jnp.zeros_like(kept).at[:, block_map].set(kept)
    return (moe_out, kv_decode)
```

```python
import jax
import jax.numpy as jnp
from jax import lax
from jax.experimental import pallas as pl
from jax.experimental.pallas import tpu as pltpu
from jax.sharding import PartitionSpec as P

LANES = 128


def passed_along(block, axis, distance):
    devices = range(lax.axis_size(axis))
    route = [((i - distance) % len(devices), i) for i in devices]
    return lax.ppermute(block, axis, route)


def rms_normed(tokens, norm_gain):
    values = tokens.astype(jnp.float32)
    scale = lax.rsqrt(jnp.mean(values * values, axis=-1, keepdims=True) + 1e-06)
    return (values * scale * norm_gain).astype(jnp.bfloat16)


def coefficients(routes, route_weights, experts):
    width = -(-experts // LANES) * LANES
    lane = jnp.arange(width, dtype=jnp.int32)
    chosen = routes[:, :, None] == lane[None, None, :]
    weights = route_weights.astype(jnp.float32)[:, :, None]
    return jnp.sum(jnp.where(chosen, weights, 0.0), axis=1).astype(jnp.bfloat16)


def placed(source, where, value):
    spot = jnp.arange(source, dtype=jnp.int32)
    hit = where[None, :] == spot[:, None]
    return jnp.sum(jnp.where(hit, value[None, :], 0), axis=1)


def sorted_order(key):
    rank = jnp.sum((key[None, :] < key[:, None]).astype(jnp.int32), axis=1)
    return rank


def pick_kernel(order_ref, empty_ref, block_ref, out_ref):
    i = pl.program_id(0)
    empty = empty_ref[order_ref[i]]
    out_ref[...] = jnp.where(empty == 1, jnp.zeros_like(block_ref[...]), block_ref[...]).reshape(
        out_ref.shape
    )


def pick_blocks(kv_prefill, order, block_empty):
    layers, blocks, block_rows, kv_width = kv_prefill.shape
    return pl.pallas_call(
        pick_kernel,
        out_shape=jax.ShapeDtypeStruct((blocks, layers, block_rows, kv_width), kv_prefill.dtype),
        grid_spec=pltpu.PrefetchScalarGridSpec(
            num_scalar_prefetch=2,
            grid=(blocks,),
            in_specs=[
                pl.BlockSpec((layers, 1, block_rows, kv_width), lambda i, o, e: (0, o[i], 0, 0))
            ],
            out_specs=pl.BlockSpec(
                (1, layers, block_rows, kv_width), lambda i, o, e: (i, 0, 0, 0)
            ),
        ),
    )(order, block_empty, kv_prefill)


def put_kernel(slot_ref, block_ref, out_ref):
    out_ref[...] = block_ref[...].reshape(out_ref.shape)


def put_blocks(arrived, slots):
    blocks, layers, block_rows, kv_width = arrived.shape
    return pl.pallas_call(
        put_kernel,
        out_shape=jax.ShapeDtypeStruct((layers, blocks, block_rows, kv_width), arrived.dtype),
        grid_spec=pltpu.PrefetchScalarGridSpec(
            num_scalar_prefetch=1,
            grid=(blocks,),
            in_specs=[
                pl.BlockSpec((1, layers, block_rows, kv_width), lambda i, s: (i, 0, 0, 0))
            ],
            out_specs=pl.BlockSpec(
                (layers, 1, block_rows, kv_width), lambda i, s: (0, s[i], 0, 0)
            ),
        ),
    )(slots, arrived)


def outgoing_blocks(kv_prefill, block_map, block_empty):
    blocks = kv_prefill.shape[1]
    exp_count = lax.axis_size("exp")
    place = jnp.arange(blocks, dtype=jnp.int32)
    peer = block_map // blocks // exp_count
    rank = sorted_order(peer * blocks + place)
    order = placed(blocks, rank, place)
    targets = placed(blocks, rank, block_map % blocks)
    return pick_blocks(kv_prefill, order, block_empty), targets


def relayout(kv_prefill, block_map, block_empty):
    blocks = kv_prefill.shape[1]
    seq_count = lax.axis_size("seq")
    per_peer = blocks // seq_count
    outgoing, targets = outgoing_blocks(kv_prefill, block_map, block_empty)
    my_seq = lax.axis_index("seq")
    arrived, tags = outgoing, targets
    for step in range(1, seq_count):
        ahead = (my_seq + step) % seq_count
        piece = lax.dynamic_slice_in_dim(outgoing, ahead * per_peer, per_peer, 0)
        label = lax.dynamic_slice_in_dim(targets, ahead * per_peer, per_peer, 0)
        piece, label = passed_along((piece, label), "seq", step)
        behind = (my_seq - step + seq_count) % seq_count
        arrived = lax.dynamic_update_slice_in_dim(arrived, piece, behind * per_peer, 0)
        tags = lax.dynamic_update_slice_in_dim(tags, label, behind * per_peer, 0)
    return put_blocks(arrived, tags)


def dense_experts(rows, coef, w_gate, w_up, w_down):
    total = None
    for e in range(w_gate.shape[0]):
        gate = jnp.dot(rows, w_gate[e], preferred_element_type=jnp.float32)
        upward = jnp.dot(rows, w_up[e], preferred_element_type=jnp.float32)
        hidden = jax.nn.silu(gate) * upward * coef[:, e : e + 1].astype(jnp.float32)
        part = jnp.dot(
            hidden.astype(jnp.bfloat16), w_down[e], preferred_element_type=jnp.float32
        )
        total = part if total is None else total + part
    return total.astype(jnp.bfloat16)


def plain(packed, w_gate, w_up, w_down):
    width = w_gate.shape[1]
    local_experts = w_gate.shape[0]
    everyone = lax.all_gather(packed, "exp", axis=0, tiled=True)
    rows = everyone[:, :width]
    coef = lax.dynamic_slice_in_dim(
        everyone[:, width:], lax.axis_index("exp") * local_experts, local_experts, 1
    )
    partial_value = dense_experts(rows, coef, w_gate, w_up, w_down)
    held = lax.psum_scatter(partial_value, "seq", scatter_dimension=1, tiled=True)
    return lax.psum_scatter(held, "exp", scatter_dimension=0, tiled=True)


def per_device(
    tokens,
    norm_gain,
    routes,
    route_weights,
    w_gate,
    w_up,
    w_down,
    kv_prefill,
    block_map,
    block_empty,
):
    experts = w_gate.shape[0] * lax.axis_size("exp")
    normed = rms_normed(tokens, norm_gain)
    packed = jnp.concatenate([normed, coefficients(routes, route_weights, experts)], axis=1)
    half = packed.shape[0] // 2
    mixed = jnp.concatenate(
        [plain(packed[i : i + half], w_gate, w_up, w_down) for i in (0, half)], axis=0
    )
    kv_decode = relayout(kv_prefill, block_map, block_empty)
    return (mixed, kv_decode)


def solution(mesh):
    in_specs = (
        P("exp", None),
        P(),
        P("exp", None),
        P("exp", None),
        P("exp", None, "seq"),
        P("exp", None, "seq"),
        P("exp", "seq", None),
        P(None, ("seq", "exp"), None, None),
        P(("seq", "exp")),
        P(("seq", "exp")),
    )
    out_specs = (P("exp", "seq"), P(None, ("seq", "exp"), None, None))
    return jax.shard_map(
        per_device, mesh=mesh, in_specs=in_specs, out_specs=out_specs, check_vma=False
    )
```

```python
import jax
import jax.numpy as jnp
from jax import lax
from jax.experimental import pallas as pl
from jax.experimental.pallas import tpu as pltpu
from jax.sharding import PartitionSpec as P

LANES = 128


def passed_along(block, axis, distance):
    devices = range(lax.axis_size(axis))
    route = [((i - distance) % len(devices), i) for i in devices]
    return lax.ppermute(block, axis, route)


def rms_normed(tokens, norm_gain):
    values = tokens.astype(jnp.float32)
    scale = lax.rsqrt(jnp.mean(values * values, axis=-1, keepdims=True) + 1e-06)
    return (values * scale * norm_gain).astype(jnp.bfloat16)


def coefficients(routes, route_weights, experts):
    width = -(-experts // LANES) * LANES
    lane = jnp.arange(width, dtype=jnp.int32)
    chosen = routes[:, :, None] == lane[None, None, :]
    weights = route_weights.astype(jnp.float32)[:, :, None]
    return jnp.sum(jnp.where(chosen, weights, 0.0), axis=1).astype(jnp.bfloat16)


def placed(source, where, value):
    spot = jnp.arange(source, dtype=jnp.int32)
    hit = where[None, :] == spot[:, None]
    return jnp.sum(jnp.where(hit, value[None, :], 0), axis=1)


def sorted_order(key):
    rank = jnp.sum((key[None, :] < key[:, None]).astype(jnp.int32), axis=1)
    return rank


def pick_kernel(order_ref, empty_ref, block_ref, out_ref):
    i = pl.program_id(0)
    empty = empty_ref[order_ref[i]]
    out_ref[...] = jnp.where(empty == 1, jnp.zeros_like(block_ref[...]), block_ref[...]).reshape(
        out_ref.shape
    )


def pick_blocks(kv_prefill, order, block_empty):
    layers, blocks, block_rows, kv_width = kv_prefill.shape
    return pl.pallas_call(
        pick_kernel,
        out_shape=jax.ShapeDtypeStruct((blocks, layers, block_rows, kv_width), kv_prefill.dtype),
        grid_spec=pltpu.PrefetchScalarGridSpec(
            num_scalar_prefetch=2,
            grid=(blocks,),
            in_specs=[
                pl.BlockSpec((layers, 1, block_rows, kv_width), lambda i, o, e: (0, o[i], 0, 0))
            ],
            out_specs=pl.BlockSpec(
                (1, layers, block_rows, kv_width), lambda i, o, e: (i, 0, 0, 0)
            ),
        ),
    )(order, block_empty, kv_prefill)


def put_kernel(slot_ref, block_ref, out_ref):
    out_ref[...] = block_ref[...].reshape(out_ref.shape)


def put_blocks(arrived, slots):
    blocks, layers, block_rows, kv_width = arrived.shape
    return pl.pallas_call(
        put_kernel,
        out_shape=jax.ShapeDtypeStruct((layers, blocks, block_rows, kv_width), arrived.dtype),
        grid_spec=pltpu.PrefetchScalarGridSpec(
            num_scalar_prefetch=1,
            grid=(blocks,),
            in_specs=[
                pl.BlockSpec((1, layers, block_rows, kv_width), lambda i, s: (i, 0, 0, 0))
            ],
            out_specs=pl.BlockSpec(
                (layers, 1, block_rows, kv_width), lambda i, s: (0, s[i], 0, 0)
            ),
        ),
    )(slots, arrived)


def outgoing_blocks(kv_prefill, block_map, block_empty):
    blocks = kv_prefill.shape[1]
    exp_count = lax.axis_size("exp")
    place = jnp.arange(blocks, dtype=jnp.int32)
    peer = block_map // blocks // exp_count
    rank = sorted_order(peer * blocks + place)
    order = placed(blocks, rank, place)
    targets = placed(blocks, rank, block_map % blocks)
    return pick_blocks(kv_prefill, order, block_empty), targets


def relayout(kv_prefill, block_map, block_empty):
    blocks = kv_prefill.shape[1]
    seq_count = lax.axis_size("seq")
    per_peer = blocks // seq_count
    outgoing, targets = outgoing_blocks(kv_prefill, block_map, block_empty)
    my_seq = lax.axis_index("seq")
    arrived, tags = outgoing, targets
    for step in range(1, seq_count):
        ahead = (my_seq + step) % seq_count
        piece = lax.dynamic_slice_in_dim(outgoing, ahead * per_peer, per_peer, 0)
        label = lax.dynamic_slice_in_dim(targets, ahead * per_peer, per_peer, 0)
        piece, label = passed_along((piece, label), "seq", step)
        behind = (my_seq - step + seq_count) % seq_count
        arrived = lax.dynamic_update_slice_in_dim(arrived, piece, behind * per_peer, 0)
        tags = lax.dynamic_update_slice_in_dim(tags, label, behind * per_peer, 0)
    return put_blocks(arrived, tags)


def dense_experts(rows, coef, w_gate, w_up, w_down):
    total = None
    for e in range(w_gate.shape[0]):
        gate = jnp.dot(rows, w_gate[e], preferred_element_type=jnp.float32)
        upward = jnp.dot(rows, w_up[e], preferred_element_type=jnp.float32)
        hidden = jax.nn.silu(gate) * upward * coef[:, e : e + 1].astype(jnp.float32)
        part = jnp.dot(
            hidden.astype(jnp.bfloat16), w_down[e], preferred_element_type=jnp.float32
        )
        total = part if total is None else total + part
    return total.astype(jnp.bfloat16)


def plain(packed, w_gate, w_up, w_down):
    width = w_gate.shape[1]
    local_experts = w_gate.shape[0]
    everyone = lax.all_gather(packed, "exp", axis=0, tiled=True)
    rows = everyone[:, :width]
    coef = lax.dynamic_slice_in_dim(
        everyone[:, width:], lax.axis_index("exp") * local_experts, local_experts, 1
    )
    partial_value = dense_experts(rows, coef, w_gate, w_up, w_down)
    held = lax.psum_scatter(partial_value, "seq", scatter_dimension=1, tiled=True)
    return lax.psum_scatter(held, "exp", scatter_dimension=0, tiled=True)


def fused_kernel(
    packed_ref,
    w_gate_ref,
    w_up_ref,
    w_down_ref,
    kv_ref,
    label_ref,
    out_ref,
    arrived_ref,
    tag_ref,
    held,
    gate_w,
    up_w,
    down_w,
    hidden,
    part,
    pair,
    slices,
    summed,
    columns,
    local_sem,
    z_send,
    z_recv,
    row_send,
    row_recv,
    core_send,
    core_recv,
    pair_send,
    pair_recv,
    slice_send,
    slice_recv,
    sum_send,
    sum_recv,
    kv_send,
    kv_recv,
    label_send,
    label_recv,
):
    local_experts, width, ff = w_gate_ref.shape
    n_z, n_seq = slices.shape[0], slices.shape[1]
    tokens = packed_ref.shape[0]
    quarter = tokens // n_seq
    per_peer = kv_ref.shape[0] // n_seq
    seq = lax.axis_index("seq")
    me = lax.axis_index("exp")
    z, core = me // 2, lax.rem(me, 2)

    def remote(src, dst, send, recv, to_seq, to_exp):
        return pltpu.make_async_remote_copy(
            src_ref=src,
            dst_ref=dst,
            send_sem=send,
            recv_sem=recv,
            device_id={"seq": to_seq, "exp": to_exp},
            device_id_type=pl.DeviceIdType.MESH,
        )

    loads = []
    for e in range(local_experts):
        spot = pl.ds(e * ff, ff)
        loads.append((w_gate_ref.at[e], gate_w.at[:, spot]))
        loads.append((w_up_ref.at[e], up_w.at[:, spot]))
        loads.append((w_down_ref.at[e], down_w.at[spot]))
    mine = pl.ds(seq * per_peer, per_peer)
    loads.append((kv_ref.at[mine], arrived_ref.at[mine]))
    loads.append((label_ref.at[seq], tag_ref.at[seq]))
    loads = [pltpu.make_async_copy(a, b, local_sem.at[i]) for i, (a, b) in enumerate(loads)]
    for load in loads:
        load.start()

    def other_z(d):
        return lax.rem(z + d, n_z)

    def other_seq(d):
        return lax.rem(seq + d, n_seq)

    sibling = z * 2 + 1 - core
    barrier = pltpu.get_barrier_semaphore()
    pl.semaphore_signal(
        barrier, 1, device_id={"seq": seq, "exp": sibling}, device_id_type=pl.DeviceIdType.MESH
    )
    for d in range(1, n_z):
        pl.semaphore_signal(
            barrier,
            1,
            device_id={"seq": seq, "exp": other_z(d) * 2 + core},
            device_id_type=pl.DeviceIdType.MESH,
        )
    for d in range(1, n_seq):
        pl.semaphore_signal(
            barrier,
            1,
            device_id={"seq": other_seq(d), "exp": me},
            device_id_type=pl.DeviceIdType.MESH,
        )
    held[me] = packed_ref[...]
    pl.semaphore_wait(barrier, n_z + n_seq - 1)

    own_rows = pl.ds(seq * quarter, quarter)

    def to_z(d):
        rows = held.at[me, own_rows]
        return remote(rows, rows, z_send.at[d], z_recv.at[z], seq, other_z(d) * 2 + core)

    def from_z(zs):
        rows = held.at[zs * 2 + core, own_rows]
        return remote(rows, rows, z_send.at[0], z_recv.at[zs], seq, sibling)

    def to_row(zs, d):
        rows = held.at[zs * 2 + core, own_rows]
        return remote(
            rows, rows, row_send.at[zs, d], row_recv.at[zs, seq], other_seq(d), me
        )

    def from_row(zs, peer):
        rows = held.at[zs * 2 + core, pl.ds(peer * quarter, quarter)]
        return remote(rows, rows, row_send.at[0, 0], row_recv.at[zs, peer], seq, sibling)

    def to_core(zs):
        block = held.at[zs * 2 + core]
        return remote(block, block, core_send.at[zs], core_recv.at[zs], seq, sibling)

    def from_core(zs):
        block = held.at[zs * 2 + 1 - core]
        return remote(block, block, core_send.at[0], core_recv.at[zs], seq, sibling)

    def to_pair(zs):
        return remote(part.at[1, zs], pair.at[zs], pair_send.at[zs], pair_recv.at[zs], seq, sibling)

    def to_slice(zs, d):
        peer = other_seq(d)
        return remote(
            part.at[0, zs, peer],
            slices.at[zs, seq],
            slice_send.at[zs, d],
            slice_recv.at[zs, seq],
            peer,
            me,
        )

    def from_slice(zs, peer):
        spot = slices.at[zs, peer]
        return remote(spot, spot, slice_send.at[0, 0], slice_recv.at[zs, peer], seq, sibling)

    def to_sum(zs):
        return remote(
            summed.at[zs], columns.at[z], sum_send.at[zs], sum_recv.at[z], seq, zs * 2 + core
        )

    def from_sum(zs):
        spot = columns.at[zs]
        return remote(spot, spot, sum_send.at[0], sum_recv.at[zs], seq, sibling)

    def to_kv(d):
        peer = other_seq(d)
        return remote(
            kv_ref.at[pl.ds(peer * per_peer, per_peer)],
            arrived_ref.at[mine],
            kv_send.at[d],
            kv_recv.at[seq],
            peer,
            me,
        )

    def from_kv(peer):
        spot = arrived_ref.at[pl.ds(peer * per_peer, per_peer)]
        return remote(spot, spot, kv_send.at[0], kv_recv.at[peer], seq, sibling)

    def to_label(d):
        peer = other_seq(d)
        return remote(
            label_ref.at[peer], tag_ref.at[seq], label_send.at[d], label_recv.at[seq], peer, me
        )

    def from_label(peer):
        spot = tag_ref.at[peer]
        return remote(spot, spot, label_send.at[0], label_recv.at[peer], seq, sibling)

    for d in range(1, n_z):
        to_z(d).start()
    to_core(z).start()
    for d in range(1, n_seq):
        to_kv(d).start()
        to_label(d).start()
    for load in loads:
        load.wait()

    def compute(block, j, zs):
        rows = held[block, :, :width]
        coef = held[block, :, width:].astype(jnp.float32)
        lane = lax.broadcasted_iota(jnp.int32, coef.shape, 1)
        gate = jnp.dot(rows, gate_w[...], preferred_element_type=jnp.float32)
        upward = jnp.dot(rows, up_w[...], preferred_element_type=jnp.float32)
        value = gate / (1.0 + jnp.exp(-gate)) * upward
        for e in range(local_experts):
            scale = jnp.sum(
                jnp.where(lane == me * local_experts + e, coef, 0.0), axis=1, keepdims=True
            )
            spot = slice(e * ff, (e + 1) * ff)
            hidden[:, spot] = (value[:, spot] * scale).astype(hidden.dtype)
        out_width = part.shape[-1]
        for s in range(n_seq):
            down = down_w[:, s * out_width : (s + 1) * out_width]
            part[j, zs, s] = jnp.dot(
                hidden[...], down, preferred_element_type=jnp.float32
            ).astype(part.dtype)

    def finish_seq(zs):
        total = part[0, zs, seq].astype(jnp.float32)
        for d in range(1, n_seq):
            peer = other_seq(d)
            from_slice(zs, peer).wait_recv()
            total = total + slices[zs, peer].astype(jnp.float32)
        summed[zs] = total.astype(summed.dtype)

    def step(k, carry):
        zs = other_z(k)

        @pl.when(k > 0)
        def _():
            for d in range(1, n_seq):
                from_row(zs, other_seq(d)).wait_recv()
            to_core(zs).start()

        def half(j, inner):
            @pl.when(j == 1)
            def _():
                from_core(zs).wait_recv()

            compute(zs * 2 + lax.rem(core + j, 2), j, zs)
            return inner

        lax.fori_loop(0, 2, half, 0)
        to_pair(zs).start()

        @pl.when(k == 0)
        def _():
            for d in range(1, n_z):
                source = other_z(d)
                from_z(source).wait_recv()
                for p in range(1, n_seq):
                    to_row(source, p).start()

        to_pair(zs).wait_recv()
        for s in range(n_seq):
            both = part[0, zs, s].astype(jnp.float32) + pair[zs, s].astype(jnp.float32)
            part[0, zs, s] = both.astype(part.dtype)
        for d in range(1, n_seq):
            to_slice(zs, d).start()

        @pl.when(k > 1)
        def _():
            earlier = other_z(k - 1)
            finish_seq(earlier)
            to_sum(earlier).start()

        return carry

    lax.fori_loop(0, n_z, step, 0)
    if n_z > 1:
        last = other_z(n_z - 1)
        finish_seq(last)
        to_sum(last).start()
    finish_seq(z)
    total = summed[z].astype(jnp.float32)
    for d in range(1, n_z):
        source = other_z(d)
        from_sum(source).wait_recv()
        total = total + columns[source].astype(jnp.float32)
    out_ref[...] = total.astype(out_ref.dtype)

    for d in range(1, n_seq):
        from_kv(other_seq(d)).wait_recv()
        from_label(other_seq(d)).wait_recv()
        to_kv(d).wait_send()
        to_label(d).wait_send()
    for d in range(1, n_z):
        to_z(d).wait_send()
        to_sum(other_z(d)).wait_send()
    for d in range(n_z):
        zs = other_z(d)
        to_core(zs).wait_send()
        to_pair(zs).wait_send()
        for p in range(1, n_seq):
            to_slice(zs, p).wait_send()
            if d > 0:
                to_row(zs, p).wait_send()


def fused_bytes(packed, w_gate, n_z, n_seq):
    tokens, full = packed.shape
    experts, width, ff = w_gate.shape
    values = (2 * n_z + 1) * tokens * full + 3 * experts * width * ff + tokens * experts * ff
    return 2 * (values + 4 * n_z * tokens * width + (2 * n_z + 1) * tokens * width // n_seq)


def fused(packed, w_gate, w_up, w_down, kv_out, labels, n_z, n_seq):
    tokens, full = packed.shape
    experts, width, ff = w_gate.shape
    out_width = width // n_seq
    hid = experts * ff
    bf16 = jnp.bfloat16
    dma = pltpu.SemaphoreType.DMA
    hbm = pl.BlockSpec(memory_space=pl.ANY)
    vmem = pl.BlockSpec(memory_space=pltpu.VMEM)
    return pl.pallas_call(
        fused_kernel,
        out_shape=(
            jax.ShapeDtypeStruct((tokens, out_width), bf16),
            jax.ShapeDtypeStruct(kv_out.shape, kv_out.dtype),
            jax.ShapeDtypeStruct(labels.shape, labels.dtype),
        ),
        in_specs=[vmem, hbm, hbm, hbm, hbm, hbm],
        out_specs=(vmem, hbm, hbm),
        scratch_shapes=[
            pltpu.VMEM((2 * n_z, tokens, full), bf16),
            pltpu.VMEM((width, hid), bf16),
            pltpu.VMEM((width, hid), bf16),
            pltpu.VMEM((hid, width), bf16),
            pltpu.VMEM((tokens, hid), bf16),
            pltpu.VMEM((2, n_z, n_seq, tokens, out_width), bf16),
            pltpu.VMEM((n_z, n_seq, tokens, out_width), bf16),
            pltpu.VMEM((n_z, n_seq, tokens, out_width), bf16),
            pltpu.VMEM((n_z, tokens, out_width), bf16),
            pltpu.VMEM((n_z, tokens, out_width), bf16),
            dma((3 * experts + 2,)),
            dma((n_z,)),
            dma((n_z,)),
            dma((n_z, n_seq)),
            dma((n_z, n_seq)),
            dma((n_z,)),
            dma((n_z,)),
            dma((n_z,)),
            dma((n_z,)),
            dma((n_z, n_seq)),
            dma((n_z, n_seq)),
            dma((n_z,)),
            dma((n_z,)),
            dma((n_seq,)),
            dma((n_seq,)),
            dma((n_seq,)),
            dma((n_seq,)),
        ],
        compiler_params=pltpu.CompilerParams(
            collective_id=0, has_side_effects=True, vmem_limit_bytes=60 * 2**20
        ),
    )(packed, w_gate, w_up, w_down, kv_out, labels)


def per_device(
    tokens,
    norm_gain,
    routes,
    route_weights,
    w_gate,
    w_up,
    w_down,
    kv_prefill,
    block_map,
    block_empty,
):
    experts = w_gate.shape[0] * lax.axis_size("exp")
    normed = rms_normed(tokens, norm_gain)
    packed = jnp.concatenate([normed, coefficients(routes, route_weights, experts)], axis=1)
    n_exp, n_seq = lax.axis_size("exp"), lax.axis_size("seq")
    lanes_fit = normed.shape[1] // n_seq % LANES == 0 and w_gate.shape[2] % LANES == 0
    rows_fit = packed.shape[0] // n_seq % 16 == 0 and n_exp % 2 == 0
    if lanes_fit and rows_fit and fused_bytes(packed, w_gate, n_exp // 2, n_seq) < 54 * 2**20:
        kv_out, targets = outgoing_blocks(kv_prefill, block_map, block_empty)
        blocks = targets.shape[0]
        per_peer = blocks // n_seq
        labels = jnp.zeros((n_seq, -(-per_peer // 8) * 8, LANES), jnp.int32)
        labels = labels + jnp.pad(
            targets.reshape(n_seq, per_peer, 1), ((0, 0), (0, labels.shape[1] - per_peer), (0, 0))
        )
        mixed, arrived, tags = fused(
            packed, w_gate, w_up, w_down, kv_out, labels, n_exp // 2, n_seq
        )
        return (mixed, put_blocks(arrived, tags[:, :per_peer, 0].reshape(blocks)))
    half = packed.shape[0] // 2
    mixed = jnp.concatenate(
        [plain(packed[i : i + half], w_gate, w_up, w_down) for i in (0, half)], axis=0
    )
    kv_decode = relayout(kv_prefill, block_map, block_empty)
    return (mixed, kv_decode)


def solution(mesh):
    in_specs = (
        P("exp", None),
        P(),
        P("exp", None),
        P("exp", None),
        P("exp", None, "seq"),
        P("exp", None, "seq"),
        P("exp", "seq", None),
        P(None, ("seq", "exp"), None, None),
        P(("seq", "exp")),
        P(("seq", "exp")),
    )
    out_specs = (P("exp", "seq"), P(None, ("seq", "exp"), None, None))
    return jax.shard_map(
        per_device, mesh=mesh, in_specs=in_specs, out_specs=out_specs, check_vma=False
    )
```
